32 devices in a mesh: seq: 16 (over z, y, x), hid: 2 (over core).
Axes of the slice: x: 2, y: 2, z: 4, core: 2. Of those that a mesh axis runs over, the one named last changes fastest.
Arguments:
- tokens: bfloat16 [256, 6144], P('seq'), may hold values from -6 to 6
- out_grad: bfloat16 [256, 6144], P('seq'), may hold values from -6 to 6
- expert_ids: int32 [256, 2], P('seq'), may hold values from 0 to 7, all different within a row; in each aligned block of 16 rows (0 to 15, 16 to 31, ...) at most 5 rows name the same one
- route_probs: bfloat16 [256, 2], P('seq'), may hold values from 0.099609375 to 1
- w_gate: bfloat16 [6144, 32768], P(None, ('seq', 'hid')), may hold values from -0.078125 to 0.078125
- w_up: bfloat16 [6144, 32768], P(None, ('seq', 'hid')), may hold values from -0.078125 to 0.078125
- w_down: bfloat16 [32768, 6144], P(('seq', 'hid')), may hold values from -0.046875 to 0.046875
Outputs:
- grad_tokens: bfloat16 [256, 6144], P('seq', 'hid')
- grad_gate: bfloat16 [6144, 32768], P(None, ('seq', 'hid'))
- grad_up: bfloat16 [6144, 32768], P(None, ('seq', 'hid'))
- grad_down: bfloat16 [32768, 6144], P(('seq', 'hid'))
The draws below stay inside these ranges and needn't reach their ends.
Inputs may be any that keep to these rules, and one draw needn't show every extreme that they name: `expert_ids`: within the rows of one index of seq, no expert is chosen by more than 5 rows, and some expert is chosen by exactly 5 of them in some such block.
All inputs are finite; a program needn't handle non-finite values.
Results may differ from the reference program's by a relative error of at most 0.005.
Values may be sent and summed in bfloat16 or wider, within the bound.
A program may use at most 128 MiB of HBM per device.

```python
import math
import jax
import jax.numpy as jnp
import numpy as np
from jax import lax

D = 6144
FF = 16384
EXPERTS = 8
TOPK = 2
EXP_WIN = 2
MOST = 5
TOK_DEV = 16
TOKENS = 256


def block_scale(own_key, shape, split, least, largest):
    gain, own = 1.0, jax.random.fold_in(own_key, 6)
    for position, blocks in split:
        draws = jnp.exp(jax.random.uniform(jax.random.fold_in(own, position), (blocks,), jnp.float32, least / len(split), largest / len(split)))
        gain = gain * jnp.repeat(draws, shape[position] // blocks).reshape([-1 if axis == position else 1 for axis in range(len(shape))])
    return gain


def routed_block(rng, own, number, rows, number_of, top, bound, slope):
    ranking = jax.random.permutation(rng, number_of)
    crowded, common = shares(number_of, rows * top, bound, slope, True), shares(number_of, rows * top, bound, slope, False)
    places = jnp.arange(number_of)

    def named(sizes, turn):
        used = int((sizes > 0).sum())
        fixed = max(1, used // 4)
        passed = fixed + (places - fixed + turn * (used - fixed)) % max(1, number_of - fixed)
        return jnp.zeros((number_of,), jnp.int32).at[ranking[jnp.where(places < fixed, places, passed)]].set(jnp.asarray(sizes, jnp.int32))

    sizes = jnp.where(number % 4 == 0, named(crowded, number // 4), named(common, number - number // 4 - 1))
    mixed = jax.random.permutation(jax.random.fold_in(own, 3), number_of)
    donor, receiver = mixed[0:number_of // 2 * 2:2], mixed[1:number_of // 2 * 2:2]
    slack = jnp.minimum(sizes[donor] - 1, bound - sizes[receiver]) // 2
    slack = jnp.where((donor == ranking[0]) | (receiver == ranking[0]) | (sizes[receiver] == 0), 0, jnp.maximum(slack, 0))
    passed = jax.random.randint(jax.random.fold_in(own, 4), (number_of // 2,), 0, 1 << 20) % (slack + 1)
    sizes = sizes.at[donor].add(-passed).at[receiver].add(passed)
    labels = jnp.searchsorted(jnp.cumsum(sizes), jnp.arange(rows * top), side="right").astype(jnp.int32)
    listing = labels.reshape(top, rows).T
    listing = listing[jax.random.permutation(jax.random.fold_in(own, 1), rows)]
    turn = jax.random.randint(jax.random.fold_in(own, 2), (rows, 1), 0, top)
    return jnp.take_along_axis(listing, (jnp.arange(top)[None, :] + turn) % top, axis=1)


def shares(amount, total, limit, slope, full):
    loads = [(1 << 20) // math.isqrt(rank ** slope) + 1 for rank in range(1, amount + 1)]
    largest = limit if full else min(limit, max(-(-total // amount), total * loads[0] // sum(loads)))
    least = 1 if total - largest >= amount - 1 else 0
    counts, rest = [largest] + [least] * (amount - 1), total - largest - least * (amount - 1)
    while rest > 0:
        movable = [i for i in range(1, amount) if counts[i] < largest] or [i for i in range(1, amount) if counts[i] < limit]
        pool, remaining = sum([loads[i] for i in movable]), rest
        for i in movable:
            addition = min(limit - counts[i], max(1, remaining * loads[i] // pool), rest)
            counts[i] = counts[i] + addition
            rest = rest - addition
    return np.array(counts)


def bell_draw(key, shape, scale, most, split=(), kind=jnp.bfloat16):
    result = jax.random.normal(key, shape, jnp.float32) * scale
    if len(split) > 0:
        result = block_scale(key, shape, split, -0.22, 0.18) * result
    return jnp.clip(result, min=-most, max=most).astype(kind)


def setup_inputs(seed: int = 0) -> dict:
    seeds = jax.random.split(jax.random.key(seed), 8)
    tokens = bell_draw(seeds[0], (TOKENS, D), 1.0, 6.0, ((0, 16),))
    out_grad = bell_draw(seeds[1], (TOKENS, D), 1.0, 6.0, ((0, 16),))
    expert_ids_keys = jax.random.split(jax.random.fold_in(seeds[2], 1), TOKENS // TOK_DEV)
    expert_ids_turns = jax.random.permutation(jax.random.fold_in(seeds[2], 3), TOKENS // TOK_DEV)
    expert_ids = jax.vmap(lambda own, number: routed_block(jax.random.fold_in(seeds[2], 2), own, number, TOK_DEV, EXPERTS, TOPK, MOST, 2))(expert_ids_keys, expert_ids_turns).reshape((TOKENS, TOPK))
    route_probs = jnp.clip(0.099609375 + 0.9003906 * jax.random.uniform(seeds[3], (TOKENS, TOPK), jnp.float32) ** block_scale(seeds[3], (TOKENS, TOPK), ((0, 16),), -0.2, 0.2), 0.099609375, 1.0).astype(jnp.bfloat16)
    w_gate = bell_draw(seeds[4], (D, EXP_WIN * FF), D ** -0.5, 0.078125, ((1, 32),))
    w_up = bell_draw(seeds[5], (D, EXP_WIN * FF), D ** -0.5, 0.078125, ((1, 32),))
    w_down = bell_draw(seeds[6], (EXP_WIN * FF, D), FF ** -0.5, 0.046875, ((0, 32),))
    return {"tokens": tokens, "out_grad": out_grad, "expert_ids": expert_ids, "route_probs": route_probs, "w_gate": w_gate, "w_up": w_up, "w_down": w_down}


def silu_slope(gate_pre):
    sig_gate = jax.nn.sigmoid(gate_pre)
    return sig_gate * (1.0 + gate_pre * (1.0 - sig_gate))


def expert_block(tok_rows, grad_rows, row_weight, w_gate, w_up, w_down):
    gate_pre = jnp.dot(tok_rows, w_gate, preferred_element_type=jnp.float32)
    up_pre = jnp.dot(tok_rows, w_up, preferred_element_type=jnp.float32)
    act_val = jax.nn.silu(gate_pre)
    scaled = (row_weight * act_val * up_pre).astype(jnp.bfloat16)
    back_grad = lax.dot_general(grad_rows, w_down, (((1,), (1,)), ((), ())), preferred_element_type=jnp.float32)
    hidden_grad = row_weight * back_grad
    d_gate = (hidden_grad * up_pre * silu_slope(gate_pre)).astype(jnp.bfloat16)
    d_up = (hidden_grad * act_val).astype(jnp.bfloat16)
    return d_gate, d_up, scaled


def row_contract(left, right):
    return lax.dot_general(left, right, (((0,), (0,)), ((), ())), preferred_element_type=jnp.float32)


def col_contract(left, right):
    return lax.dot_general(left, right, (((1,), (1,)), ((), ())), preferred_element_type=jnp.float32)


def reference(tokens, out_grad, expert_ids, route_probs, w_gate, w_up, w_down):
    window = jnp.arange(EXP_WIN, dtype=jnp.int32)[None, :]
    combine = jnp.zeros((tokens.shape[0], EXP_WIN), jnp.float32)
    for pick_num in range(TOPK):
        combine = combine + jnp.where(expert_ids[:, pick_num:pick_num + 1] == window,
                                      route_probs[:, pick_num:pick_num + 1].astype(jnp.float32), 0.0)
    grad_sum = jnp.zeros(tokens.shape, jnp.float32)
    gate_parts = []
    up_parts = []
    down_parts = []
    for expert in range(EXP_WIN):
        low_col = expert * FF
        w_g = w_gate[:, low_col:low_col + FF]
        w_u = w_up[:, low_col:low_col + FF]
        w_d = w_down[low_col:low_col + FF, :]
        row_weight = combine[:, expert:expert + 1]
        d_gate, d_up, scaled = expert_block(tokens, out_grad, row_weight, w_g, w_u, w_d)
        gate_parts.append(row_contract(tokens, d_gate).astype(jnp.bfloat16))
        up_parts.append(row_contract(tokens, d_up).astype(jnp.bfloat16))
        down_parts.append(row_contract(scaled, out_grad).astype(jnp.bfloat16))
        grad_sum = grad_sum + col_contract(d_gate, w_g) + col_contract(d_up, w_u)
    return (grad_sum.astype(jnp.bfloat16), jnp.concatenate(gate_parts, axis=1),
            jnp.concatenate(up_parts, axis=1), jnp.concatenate(down_parts, axis=0))
```

```python
import functools

import jax
import jax.numpy as jnp
from jax import lax
from jax.experimental import pallas as pl
from jax.experimental.pallas import tpu as pltpu
from jax.sharding import PartitionSpec as P

FF = 16384
TOPK = 2
EXP_WIN = 2
MOST = 5
LANES = 128
SLAB = 16
PIECES = 3
MESH = pl.DeviceIdType.MESH
F32 = jnp.float32
BF16 = jnp.bfloat16


def silu_slope(gate_pre):
    sig_gate = jax.nn.sigmoid(gate_pre)
    return sig_gate * (1.0 + gate_pre * (1.0 - sig_gate))


def row_contract(left, right):
    return lax.dot_general(
        left, right, (((0,), (0,)), ((), ())), preferred_element_type=F32
    )


def col_contract(left, right):
    return lax.dot_general(
        left, right, (((1,), (1,)), ((), ())), preferred_element_type=F32
    )


def dot(left, right):
    return jnp.dot(left, right, preferred_element_type=F32)


def iota(shape, axis):
    return lax.broadcasted_iota(jnp.int32, shape, axis)


def expert_block(tok_rows, grad_rows, row_weight, w_gate, w_up, w_down):
    gate_pre = dot(tok_rows, w_gate)
    up_pre = dot(tok_rows, w_up)
    act_val = jax.nn.silu(gate_pre)
    scaled = (row_weight * act_val * up_pre).astype(BF16)
    hidden_grad = row_weight * col_contract(grad_rows, w_down)
    d_gate = (hidden_grad * up_pre * silu_slope(gate_pre)).astype(BF16)
    d_up = (hidden_grad * act_val).astype(BF16)
    return (d_gate, d_up, scaled)


def plain_shards(tokens, out_grad, expert_ids, route_probs, w_gate, w_up, w_down):
    col_count = w_gate.shape[1]
    dev_block = lax.axis_index("seq") * lax.axis_size("hid") + lax.axis_index("hid")
    expert = dev_block * col_count // FF
    window = jnp.arange(EXP_WIN, dtype=jnp.int32)[None, :]
    combine = jnp.zeros((tokens.shape[0], EXP_WIN), F32)
    for pick_num in range(TOPK):
        combine = combine + jnp.where(
            expert_ids[:, pick_num : pick_num + 1] == window,
            route_probs[:, pick_num : pick_num + 1].astype(F32),
            0.0,
        )
    tok_all, grad_all, comb_all = (
        lax.all_gather(tokens, "seq", axis=0, tiled=True),
        lax.all_gather(out_grad, "seq", axis=0, tiled=True),
        lax.all_gather(combine.astype(BF16), "seq", axis=0, tiled=True),
    )
    row_weight = lax.dynamic_slice_in_dim(comb_all, expert, 1, 1).astype(F32)
    d_gate, d_up, scaled = expert_block(
        tok_all, grad_all, row_weight, w_gate, w_up, w_down
    )
    terms = col_contract(d_gate, w_gate) + col_contract(d_up, w_up)
    row_sums = lax.psum_scatter(terms, "seq", scatter_dimension=0, tiled=True)
    grad_tokens = lax.psum_scatter(row_sums, "hid", scatter_dimension=1, tiled=True)
    return (
        grad_tokens.astype(BF16),
        row_contract(tok_all, d_gate).astype(BF16),
        row_contract(tok_all, d_up).astype(BF16),
        row_contract(scaled, grad_all).astype(BF16),
    )


def unpack_rows(seq_count, piece):
    rows, packed = MOST * seq_count, SLAB * seq_count
    n, r = iota((rows, packed), 0), iota((rows, packed), 1)
    return (r == SLAB * (n % seq_count) + MOST * piece + n // seq_count).astype(BF16)


def pack_rows(seq_count, piece):
    rows, packed = MOST * seq_count, SLAB * seq_count
    r, n = iota((packed, rows), 0), iota((packed, rows), 1)
    return (r == SLAB * (n % seq_count) + MOST * piece + n // seq_count).astype(BF16)


def layer_kernel(
    group,
    tok_ref,
    grad_ref,
    ids_ref,
    probs_ref,
    wg_hbm,
    wu_hbm,
    wd_hbm,
    out_ref,
    dg_ref,
    du_ref,
    sc_ref,
    tokx_ref,
    gradx_ref,
    wg,
    wu,
    wd,
    slabs,
    mir,
    gate,
    up,
    back,
    sib_out,
    sib_in,
    packed,
    red_in,
    total,
    fin_out,
    fin_in,
    w_sem,
    mir_sem,
    gat_send,
    gat_recv,
    sib_sem,
    part_sem,
    red_send,
    red_recv,
    fin_sem,
):
    seq_count = EXP_WIN * group
    rows_own, width = tok_ref.shape
    half_width = width // 2
    piece_w = half_width // PIECES
    hidden = wg.shape[2]
    me, h = lax.axis_index("seq"), lax.axis_index("hid")
    mine, c = me // group, me % group
    other = 1 - mine
    mirror = (me + group) % seq_count
    sib = (me, 1 - h)

    def weight_copies(i):
        return (
            pltpu.make_async_copy(
                wg_hbm.at[pl.ds(i * piece_w, piece_w), :], wg.at[i], w_sem.at[0, i]
            ),
            pltpu.make_async_copy(
                wu_hbm.at[pl.ds(i * piece_w, piece_w), :], wu.at[i], w_sem.at[1, i]
            ),
            pltpu.make_async_copy(
                wd_hbm.at[:, pl.ds(pl.multiple_of(i * piece_w, LANES), piece_w)],
                wd.at[i],
                w_sem.at[2, i],
            ),
        )

    def order(t):
        return ((h + t // PIECES) % 2) * PIECES + t % PIECES

    def start_gate_up(t, _):
        copies = weight_copies(order(t))
        copies[0].start()
        copies[1].start()
        return 0

    def start_down(t, _):
        weight_copies(order(t))[2].start()
        return 0

    lax.fori_loop(0, 2 * PIECES, start_gate_up, 0)
    lax.fori_loop(0, 2 * PIECES, start_down, 0)

    barrier = pltpu.get_barrier_semaphore()

    def greet(d, _):
        pl.semaphore_signal(
            barrier,
            inc=1,
            device_id=(mine * group + (c + d) % group, h),
            device_id_type=MESH,
        )
        return 0

    lax.fori_loop(1, group, greet, 0)
    pl.semaphore_signal(barrier, inc=1, device_id=(mirror, h), device_id_type=MESH)
    pl.semaphore_signal(barrier, inc=1, device_id=sib, device_id_type=MESH)

    below = (iota((rows_own, rows_own), 1) < iota((rows_own, rows_own), 0)).astype(BF16)

    def chosen(expert):
        weight = jnp.zeros((rows_own, 1), F32)
        hit = jnp.zeros((rows_own, 1), F32)
        for pick in range(TOPK):
            same = ids_ref[:, pick : pick + 1] == expert
            hit = hit + jnp.where(same, 1.0, 0.0)
            weight = weight + jnp.where(
                same, probs_ref[:, pick : pick + 1].astype(F32), 0.0
            )
        spread = jnp.broadcast_to(hit, (rows_own, LANES)).astype(BF16)
        place = dot(below, spread)[:, 0:1]
        place = jnp.where(hit > 0.0, place, -1.0)
        return place, weight

    def picker(place, piece):
        r = iota((rows_own, SLAB), 1) - MOST * piece
        inside = (r >= 0) & (r < MOST)
        return jnp.where(inside & (r.astype(F32) == place), 1.0, 0.0).astype(BF16)

    def slab_of(x_ref, place):
        acc = jnp.zeros((SLAB, piece_w), F32)
        for piece in range(PIECES):
            start = pl.multiple_of(h * half_width + piece * piece_w, LANES)
            acc = acc + row_contract(picker(place, piece), x_ref[:, pl.ds(start, piece_w)])
        return acc

    def token_slab(place, weight):
        spot = (iota((rows_own, piece_w), 1) // LANES).astype(F32)
        line = jnp.sum(jnp.where(spot == place, weight, 0.0), axis=0, keepdims=True)
        return jnp.where(
            iota((SLAB, piece_w), 0) == SLAB - 1, line, slab_of(tok_ref, place)
        )

    place_mine, weight_mine = chosen(mine)
    place_other, weight_other = chosen(other)
    mir[0] = token_slab(place_other, weight_other).astype(BF16)
    mir[1] = slab_of(grad_ref, place_other).astype(BF16)
    own_rows = pl.ds(pl.multiple_of(2 * SLAB * c + SLAB * mine, SLAB), SLAB)
    mir_rows = pl.ds(pl.multiple_of(2 * SLAB * c + SLAB * other, SLAB), SLAB)
    slabs[0, h, own_rows, :] = token_slab(place_mine, weight_mine).astype(BF16)
    slabs[1, h, own_rows, :] = slab_of(grad_ref, place_mine).astype(BF16)

    pl.semaphore_wait(barrier, group + 1)

    def mirror_copy(a, rows):
        return pltpu.make_async_remote_copy(
            src_ref=mir.at[a],
            dst_ref=slabs.at[a, h, rows, :],
            send_sem=mir_sem.at[0, a],
            recv_sem=mir_sem.at[1, a],
            device_id=(mirror, h),
            device_id_type=MESH,
        )

    def gather_copy(a, part, d, source):
        row = 2 * SLAB * source + SLAB * (mine if part == 0 else other)
        rows = pl.ds(pl.multiple_of(row, SLAB), SLAB)
        return pltpu.make_async_remote_copy(
            src_ref=slabs.at[a, h, rows, :],
            dst_ref=slabs.at[a, h, rows, :],
            send_sem=gat_send.at[a, part, d],
            recv_sem=gat_recv.at[a, part, d],
            device_id=(mine * group + (c + d) % group, h),
            device_id_type=MESH,
        )

    def send_all(a, part):
        def step(d, _):
            gather_copy(a, part, d, c).start()
            return 0

        lax.fori_loop(1, group, step, 0)

    def receive_all(a):
        def step(d, _):
            source = (c + group - d) % group
            gather_copy(a, 0, d, source).wait_recv()
            gather_copy(a, 1, d, source).wait_recv()
            return 0

        lax.fori_loop(1, group, step, 0)

    def pair_copy(a, half):
        return pltpu.make_async_remote_copy(
            src_ref=slabs.at[a, half],
            dst_ref=slabs.at[a, half],
            send_sem=sib_sem.at[0, a],
            recv_sem=sib_sem.at[1, a],
            device_id=sib,
            device_id_type=MESH,
        )

    mirror_copy(0, own_rows).start()
    mirror_copy(1, own_rows).start()
    send_all(0, 0)
    mirror_copy(0, mir_rows).wait_recv()
    send_all(0, 1)
    send_all(1, 0)
    mirror_copy(1, mir_rows).wait_recv()
    send_all(1, 1)

    receive_all(0)
    pair_copy(0, h).start()

    rows_all = MOST * seq_count
    n, r = iota((rows_all, SLAB * seq_count), 0), iota((rows_all, SLAB * seq_count), 1)
    last = (r == SLAB * (n % seq_count) + SLAB - 1).astype(BF16)
    lines = dot(last, slabs[0, h])
    n, r = iota((rows_all, piece_w), 0), iota((rows_all, piece_w), 1)
    row_weight = jnp.sum(
        jnp.where(r == LANES * (n // seq_count), lines, 0.0), axis=1, keepdims=True
    )

    gate[...] = jnp.zeros_like(gate)
    up[...] = jnp.zeros_like(up)
    back[...] = jnp.zeros_like(back)

    def rows_of(a, i, x_ref):
        x = dot(unpack_rows(seq_count, i % PIECES), slabs[a, i // PIECES]).astype(BF16)
        x_ref[:, pl.ds(pl.multiple_of(i * piece_w, LANES), piece_w)] = x
        return x

    def forward_step(t, _):
        i = order(t)
        copies = weight_copies(i)
        x = rows_of(0, i, tokx_ref)
        copies[0].wait()
        gate[...] += dot(x, wg[i])
        copies[1].wait()
        up[...] += dot(x, wu[i])
        return 0

    def back_step(t, _):
        i = order(t)
        x = rows_of(1, i, gradx_ref)
        weight_copies(i)[2].wait()
        back[...] += col_contract(x, wd[i])
        return 0

    lax.fori_loop(0, PIECES, forward_step, 0)
    receive_all(1)
    pair_copy(1, h).start()
    pair_copy(0, 1 - h).wait_recv()
    lax.fori_loop(PIECES, 2 * PIECES, forward_step, 0)
    lax.fori_loop(0, PIECES, back_step, 0)
    pair_copy(1, 1 - h).wait_recv()
    lax.fori_loop(PIECES, 2 * PIECES, back_step, 0)

    gate_pre, up_pre = gate[...], up[...]
    sig = 1.0 / (1.0 + jnp.exp(-gate_pre))
    act = gate_pre * sig
    hidden_grad = row_weight * back[...]
    sc_ref[...] = (row_weight * act * up_pre).astype(BF16)
    dg_ref[...] = (
        hidden_grad * up_pre * (sig * (1.0 + gate_pre * (1.0 - sig)))
    ).astype(BF16)
    du_ref[...] = (hidden_grad * act).astype(BF16)

    cuts = packed.shape[0]
    cut = piece_w // cuts

    def terms(half, q, piece):
        i = half * PIECES + piece
        rows = pl.ds(pl.multiple_of(q * cut, SLAB), cut)
        return col_contract(dg_ref[...], wg[i, rows, :]) + col_contract(
            du_ref[...], wu[i, rows, :]
        )

    def part_copy(q):
        return pltpu.make_async_remote_copy(
            src_ref=sib_out.at[q],
            dst_ref=sib_in.at[q],
            send_sem=part_sem.at[0, q],
            recv_sem=part_sem.at[1, q],
            device_id=sib,
            device_id_type=MESH,
        )

    def reduce_copy(q, d):
        target = (c + d) % group
        return pltpu.make_async_remote_copy(
            src_ref=packed.at[
                q, pl.ds(pl.multiple_of(2 * SLAB * target, 2 * SLAB), 2 * SLAB), :
            ],
            dst_ref=red_in.at[q, d],
            send_sem=red_send.at[q, d],
            recv_sem=red_recv.at[q, d],
            device_id=(mine * group + target, h),
            device_id_type=MESH,
        )

    def far_step(q, _):
        for piece in range(PIECES):
            sib_out[q, piece] = terms(1 - h, q, piece).astype(BF16)
        part_copy(q).start()
        return 0

    def near_step(q, _):
        part_copy(q).wait_recv()
        acc = jnp.zeros((SLAB * seq_count, cut), F32)
        for piece in range(PIECES):
            both = terms(h, q, piece) + sib_in[q, piece].astype(F32)
            acc = acc + dot(pack_rows(seq_count, piece), both.astype(BF16))
        packed[q] = acc.astype(BF16)

        def send(d, _):
            reduce_copy(q, d).start()
            return 0

        lax.fori_loop(1, group, send, 0)
        return 0

    lax.fori_loop(0, cuts, far_step, 0)
    lax.fori_loop(0, cuts, near_step, 0)

    def final_copy(q):
        return pltpu.make_async_remote_copy(
            src_ref=fin_out.at[q],
            dst_ref=fin_in.at[q],
            send_sem=fin_sem.at[0, q],
            recv_sem=fin_sem.at[1, q],
            device_id=(mirror, h),
            device_id_type=MESH,
        )

    def sum_step(q, _):
        own = pl.ds(pl.multiple_of(2 * SLAB * c, 2 * SLAB), 2 * SLAB)
        total[q] = packed[q, own, :].astype(F32)

        def add(d, _):
            reduce_copy(q, d).wait_recv()
            total[q] += red_in[q, d].astype(F32)
            return 0

        lax.fori_loop(1, group, add, 0)
        away = pl.ds(pl.multiple_of(SLAB * other, SLAB), SLAB)
        fin_out[q] = total[q, away, :].astype(BF16)
        final_copy(q).start()
        return 0

    lax.fori_loop(0, cuts, sum_step, 0)

    stay = pl.ds(pl.multiple_of(SLAB * mine, SLAB), SLAB)
    for q in range(cuts):
        final_copy(q).wait_recv()
        near = total[q, stay, :].astype(BF16)
        far = fin_in[q]
        for piece in range(PIECES):
            value = dot(picker(place_mine, piece), near) + dot(
                picker(place_other, piece), far
            )
            out_ref[:, piece * piece_w + q * cut : piece * piece_w + (q + 1) * cut] = (
                value.astype(BF16)
            )

    for a in range(2):
        mirror_copy(a, own_rows).wait_send()
        pair_copy(a, h).wait_send()

    def sent(d, _):
        for a in range(2):
            for part in range(2):
                gather_copy(a, part, d, c).wait_send()
        for q in range(cuts):
            reduce_copy(q, d).wait_send()
        return 0

    lax.fori_loop(1, group, sent, 0)
    for q in range(cuts):
        part_copy(q).wait_send()
        final_copy(q).wait_send()


def weight_grads(tokx_ref, gradx_ref, dg_ref, du_ref, sc_ref, gg_ref, gu_ref, gd_ref):
    x = tokx_ref[...]
    gg_ref[...] = row_contract(x, dg_ref[...]).astype(BF16)
    gu_ref[...] = row_contract(x, du_ref[...]).astype(BF16)
    gd_ref[...] = row_contract(sc_ref[...], gradx_ref[...]).astype(BF16)


def paired_shards(group, tokens, out_grad, expert_ids, route_probs, w_gate, w_up, w_down):
    seq_count = EXP_WIN * group
    rows = MOST * seq_count
    width, hidden = w_gate.shape
    piece_w = width // (2 * PIECES)
    cuts = 2
    cut = piece_w // cuts
    dma = pltpu.SemaphoreType.DMA
    vmem = pl.BlockSpec(memory_space=pltpu.VMEM)
    hbm = pl.BlockSpec(memory_space=pl.ANY)
    small = jax.ShapeDtypeStruct((rows, hidden), BF16)
    wide = jax.ShapeDtypeStruct((rows, width), BF16)
    grad_tokens, d_gate, d_up, scaled, tok_x, grad_x = pl.pallas_call(
        functools.partial(layer_kernel, group),
        out_shape=(
            jax.ShapeDtypeStruct((tokens.shape[0], width // 2), BF16),
            small,
            small,
            small,
            wide,
            wide,
        ),
        in_specs=[vmem] * 4 + [hbm] * 3,
        out_specs=(vmem,) * 6,
        scratch_shapes=[
            pltpu.VMEM((2 * PIECES, piece_w, hidden), BF16),
            pltpu.VMEM((2 * PIECES, piece_w, hidden), BF16),
            pltpu.VMEM((2 * PIECES, hidden, piece_w), BF16),
            pltpu.VMEM((2, 2, SLAB * seq_count, piece_w), BF16),
            pltpu.VMEM((2, SLAB, piece_w), BF16),
            pltpu.VMEM((rows, hidden), F32),
            pltpu.VMEM((rows, hidden), F32),
            pltpu.VMEM((rows, hidden), F32),
            pltpu.VMEM((cuts, PIECES, rows, cut), BF16),
            pltpu.VMEM((cuts, PIECES, rows, cut), BF16),
            pltpu.VMEM((cuts, SLAB * seq_count, cut), BF16),
            pltpu.VMEM((cuts, group, 2 * SLAB, cut), BF16),
            pltpu.VMEM((cuts, 2 * SLAB, cut), F32),
            pltpu.VMEM((cuts, SLAB, cut), BF16),
            pltpu.VMEM((cuts, SLAB, cut), BF16),
            dma((3, 2 * PIECES)),
            dma((2, 2)),
            dma((2, 2, group)),
            dma((2, 2, group)),
            dma((2, 2)),
            dma((2, cuts)),
            dma((cuts, group)),
            dma((cuts, group)),
            dma((2, cuts)),
        ],
        compiler_params=pltpu.CompilerParams(
            collective_id=0, has_side_effects=True, vmem_limit_bytes=60 * 2**20
        ),
        cost_estimate=pl.CostEstimate(
            flops=10 * rows * width * hidden,
            bytes_accessed=6 * width * hidden,
            transcendentals=rows * hidden,
        ),
    )(tokens, out_grad, expert_ids, route_probs, w_gate, w_up, w_down)

    step = piece_w // 2
    whole = pl.BlockSpec((rows, hidden), lambda i: (0, 0))
    strip = pl.BlockSpec((rows, step), lambda i: (0, i))
    grad_gate, grad_up, grad_down = pl.pallas_call(
        weight_grads,
        grid=(width // step,),
        out_shape=(
            jax.ShapeDtypeStruct((width, hidden), BF16),
            jax.ShapeDtypeStruct((width, hidden), BF16),
            jax.ShapeDtypeStruct((hidden, width), BF16),
        ),
        in_specs=[strip, strip, whole, whole, whole],
        out_specs=(
            pl.BlockSpec((step, hidden), lambda i: (i, 0)),
            pl.BlockSpec((step, hidden), lambda i: (i, 0)),
            pl.BlockSpec((hidden, step), lambda i: (0, i)),
        ),
        compiler_params=pltpu.CompilerParams(vmem_limit_bytes=48 * 2**20),
        cost_estimate=pl.CostEstimate(
            flops=6 * rows * width * hidden,
            bytes_accessed=6 * width * hidden,
            transcendentals=0,
        ),
    )(tok_x, grad_x, d_gate, d_up, scaled)
    return grad_tokens, grad_gate, grad_up, grad_down


def solution(mesh):
    paired = mesh.shape["hid"] == 2 and mesh.shape["seq"] % EXP_WIN == 0
    if paired:
        body = functools.partial(paired_shards, mesh.shape["seq"] // EXP_WIN)
    else:
        body = plain_shards
    return jax.shard_map(
        body,
        mesh=mesh,
        in_specs=(
            P("seq", None),
            P("seq", None),
            P("seq", None),
            P("seq", None),
            P(None, ("seq", "hid")),
            P(None, ("seq", "hid")),
            P(("seq", "hid"), None),
        ),
        out_specs=(
            P("seq", "hid"),
            P(None, ("seq", "hid")),
            P(None, ("seq", "hid")),
            P(("seq", "hid"), None),
        ),
        check_vma=False,
    )
```

```python
import functools

import jax
import jax.numpy as jnp
from jax import lax
from jax.experimental import pallas as pl
from jax.experimental.pallas import tpu as pltpu
from jax.sharding import PartitionSpec as P

FF = 16384
TOPK = 2
EXP_WIN = 2
MOST = 5
LANES = 128
SLAB = 16
PIECES = 3
MESH = pl.DeviceIdType.MESH
F32 = jnp.float32
BF16 = jnp.bfloat16


def silu_slope(gate_pre):
    sig_gate = jax.nn.sigmoid(gate_pre)
    return sig_gate * (1.0 + gate_pre * (1.0 - sig_gate))


def row_contract(left, right):
    return lax.dot_general(
        left, right, (((0,), (0,)), ((), ())), preferred_element_type=F32
    )


def col_contract(left, right):
    return lax.dot_general(
        left, right, (((1,), (1,)), ((), ())), preferred_element_type=F32
    )


def dot(left, right):
    return jnp.dot(left, right, preferred_element_type=F32)


def iota(shape, axis):
    return lax.broadcasted_iota(jnp.int32, shape, axis)


def expert_block(tok_rows, grad_rows, row_weight, w_gate, w_up, w_down):
    gate_pre = dot(tok_rows, w_gate)
    up_pre = dot(tok_rows, w_up)
    act_val = jax.nn.silu(gate_pre)
    scaled = (row_weight * act_val * up_pre).astype(BF16)
    hidden_grad = row_weight * col_contract(grad_rows, w_down)
    d_gate = (hidden_grad * up_pre * silu_slope(gate_pre)).astype(BF16)
    d_up = (hidden_grad * act_val).astype(BF16)
    return (d_gate, d_up, scaled)


def plain_shards(tokens, out_grad, expert_ids, route_probs, w_gate, w_up, w_down):
    col_count = w_gate.shape[1]
    dev_block = lax.axis_index("seq") * lax.axis_size("hid") + lax.axis_index("hid")
    expert = dev_block * col_count // FF
    window = jnp.arange(EXP_WIN, dtype=jnp.int32)[None, :]
    combine = jnp.zeros((tokens.shape[0], EXP_WIN), F32)
    for pick_num in range(TOPK):
        combine = combine + jnp.where(
            expert_ids[:, pick_num : pick_num + 1] == window,
            route_probs[:, pick_num : pick_num + 1].astype(F32),
            0.0,
        )
    tok_all, grad_all, comb_all = (
        lax.all_gather(tokens, "seq", axis=0, tiled=True),
        lax.all_gather(out_grad, "seq", axis=0, tiled=True),
        lax.all_gather(combine.astype(BF16), "seq", axis=0, tiled=True),
    )
    row_weight = lax.dynamic_slice_in_dim(comb_all, expert, 1, 1).astype(F32)
    d_gate, d_up, scaled = expert_block(
        tok_all, grad_all, row_weight, w_gate, w_up, w_down
    )
    terms = col_contract(d_gate, w_gate) + col_contract(d_up, w_up)
    row_sums = lax.psum_scatter(terms, "seq", scatter_dimension=0, tiled=True)
    grad_tokens = lax.psum_scatter(row_sums, "hid", scatter_dimension=1, tiled=True)
    return (
        grad_tokens.astype(BF16),
        row_contract(tok_all, d_gate).astype(BF16),
        row_contract(tok_all, d_up).astype(BF16),
        row_contract(scaled, grad_all).astype(BF16),
    )


def unpack_rows(seq_count, piece):
    rows, packed = MOST * seq_count, SLAB * seq_count
    n, r = iota((rows, packed), 0), iota((rows, packed), 1)
    return (r == SLAB * (n % seq_count) + MOST * piece + n // seq_count).astype(BF16)


def pack_rows(seq_count, piece):
    rows, packed = MOST * seq_count, SLAB * seq_count
    r, n = iota((packed, rows), 0), iota((packed, rows), 1)
    return (r == SLAB * (n % seq_count) + MOST * piece + n // seq_count).astype(BF16)


def layer_kernel(
    group,
    tok_ref,
    grad_ref,
    ids_ref,
    probs_ref,
    wg_hbm,
    wu_hbm,
    wd_hbm,
    out_ref,
    dg_hbm,
    du_hbm,
    sc_hbm,
    tokx_hbm,
    gradx_hbm,
    dg_ref,
    du_ref,
    sc_ref,
    tokx_ref,
    gradx_ref,
    wg,
    wu,
    wd,
    slabs,
    mir,
    gate,
    up,
    back,
    sib_out,
    sib_in,
    packed,
    red_in,
    total,
    fin_out,
    fin_in,
    w_sem,
    mir_sem,
    gat_send,
    gat_recv,
    sib_sem,
    part_sem,
    red_send,
    red_recv,
    fin_sem,
    keep_sem,
):
    seq_count = EXP_WIN * group
    rows_own, width = tok_ref.shape
    half_width = width // 2
    piece_w = half_width // PIECES
    hidden = wg.shape[2]
    me, h = lax.axis_index("seq"), lax.axis_index("hid")
    mine, c = me // group, me % group
    other = 1 - mine
    mirror = (me + group) % seq_count
    sib = (me, 1 - h)

    def weight_copies(i):
        return (
            pltpu.make_async_copy(
                wg_hbm.at[pl.ds(i * piece_w, piece_w), :], wg.at[i], w_sem.at[0, i]
            ),
            pltpu.make_async_copy(
                wu_hbm.at[pl.ds(i * piece_w, piece_w), :], wu.at[i], w_sem.at[1, i]
            ),
            pltpu.make_async_copy(
                wd_hbm.at[:, pl.ds(pl.multiple_of(i * piece_w, LANES), piece_w)],
                wd.at[i],
                w_sem.at[2, i],
            ),
        )

    kept = [
        pltpu.make_async_copy(source, target, keep_sem.at[k])
        for k, (source, target) in enumerate(
            (
                (tokx_ref, tokx_hbm),
                (gradx_ref, gradx_hbm),
                (dg_ref, dg_hbm),
                (du_ref, du_hbm),
                (sc_ref, sc_hbm),
            )
        )
    ]

    def order(t):
        return ((h + t // PIECES) % 2) * PIECES + t % PIECES

    def start_gate_up(t, _):
        copies = weight_copies(order(t))
        copies[0].start()
        copies[1].start()
        return 0

    def start_down(t, _):
        weight_copies(order(t))[2].start()
        return 0

    lax.fori_loop(0, 2 * PIECES, start_gate_up, 0)
    lax.fori_loop(0, 2 * PIECES, start_down, 0)

    barrier = pltpu.get_barrier_semaphore()

    def greet(d, _):
        pl.semaphore_signal(
            barrier,
            inc=1,
            device_id=(mine * group + (c + d) % group, h),
            device_id_type=MESH,
        )
        return 0

    lax.fori_loop(1, group, greet, 0)
    pl.semaphore_signal(barrier, inc=1, device_id=(mirror, h), device_id_type=MESH)
    pl.semaphore_signal(barrier, inc=1, device_id=sib, device_id_type=MESH)

    below = (iota((rows_own, rows_own), 1) < iota((rows_own, rows_own), 0)).astype(BF16)

    diagonal = iota((rows_own, rows_own), 1) == iota((rows_own, rows_own), 0)

    def chosen(expert):
        same = ids_ref[...] == expert
        hit_line = jnp.sum(jnp.where(same, 1.0, 0.0), axis=0, keepdims=True)
        weight_line = jnp.sum(
            jnp.where(same, probs_ref[...].astype(F32), 0.0), axis=0, keepdims=True
        )
        hit = jnp.sum(jnp.where(diagonal, hit_line, 0.0), axis=1, keepdims=True)
        weight = jnp.sum(jnp.where(diagonal, weight_line, 0.0), axis=1, keepdims=True)
        spread = jnp.broadcast_to(hit, (rows_own, LANES)).astype(BF16)
        place = dot(below, spread)[:, 0:1]
        place = jnp.where(hit > 0.0, place, -1.0)
        return place, weight

    def picker(place, piece):
        r = iota((rows_own, SLAB), 1) - MOST * piece
        inside = (r >= 0) & (r < MOST)
        return jnp.where(inside & (r.astype(F32) == place), 1.0, 0.0).astype(BF16)

    def slab_of(x_ref, place):
        acc = jnp.zeros((SLAB, piece_w), F32)
        for piece in range(PIECES):
            start = pl.multiple_of(h * half_width + piece * piece_w, LANES)
            acc = acc + row_contract(picker(place, piece), x_ref[:, pl.ds(start, piece_w)])
        return acc

    def token_slab(place, weight):
        spot = (iota((rows_own, piece_w), 1) // LANES).astype(F32)
        line = jnp.sum(jnp.where(spot == place, weight, 0.0), axis=0, keepdims=True)
        return jnp.where(
            iota((SLAB, piece_w), 0) == SLAB - 1, line, slab_of(tok_ref, place)
        )

    place_mine, weight_mine = chosen(mine)
    place_other, weight_other = chosen(other)
    mir[0] = token_slab(place_other, weight_other).astype(BF16)
    own_rows = pl.ds(pl.multiple_of(2 * SLAB * c + SLAB * mine, SLAB), SLAB)
    mir_rows = pl.ds(pl.multiple_of(2 * SLAB * c + SLAB * other, SLAB), SLAB)
    slabs[0, h, own_rows, :] = token_slab(place_mine, weight_mine).astype(BF16)

    pl.semaphore_wait(barrier, group + 1)

    def mirror_copy(a, rows):
        return pltpu.make_async_remote_copy(
            src_ref=mir.at[a],
            dst_ref=slabs.at[a, h, rows, :],
            send_sem=mir_sem.at[0, a],
            recv_sem=mir_sem.at[1, a],
            device_id=(mirror, h),
            device_id_type=MESH,
        )

    def gather_copy(a, part, d, source):
        row = 2 * SLAB * source + SLAB * (mine if part == 0 else other)
        rows = pl.ds(pl.multiple_of(row, SLAB), SLAB)
        return pltpu.make_async_remote_copy(
            src_ref=slabs.at[a, h, rows, :],
            dst_ref=slabs.at[a, h, rows, :],
            send_sem=gat_send.at[a, part, d],
            recv_sem=gat_recv.at[a, part, d],
            device_id=(mine * group + (c + d) % group, h),
            device_id_type=MESH,
        )

    def send_all(a, part):
        def step(d, _):
            gather_copy(a, part, d, c).start()
            return 0

        lax.fori_loop(1, group, step, 0)

    def receive_all(a):
        def step(d, _):
            source = (c + group - d) % group
            gather_copy(a, 0, d, source).wait_recv()
            gather_copy(a, 1, d, source).wait_recv()
            return 0

        lax.fori_loop(1, group, step, 0)

    def pair_copy(a, half):
        return pltpu.make_async_remote_copy(
            src_ref=slabs.at[a, half],
            dst_ref=slabs.at[a, half],
            send_sem=sib_sem.at[0, a],
            recv_sem=sib_sem.at[1, a],
            device_id=sib,
            device_id_type=MESH,
        )

    mirror_copy(0, own_rows).start()
    send_all(0, 0)
    mir[1] = slab_of(grad_ref, place_other).astype(BF16)
    mirror_copy(1, own_rows).start()
    slabs[1, h, own_rows, :] = slab_of(grad_ref, place_mine).astype(BF16)
    mirror_copy(0, mir_rows).wait_recv()
    send_all(0, 1)
    send_all(1, 0)
    mirror_copy(1, mir_rows).wait_recv()
    send_all(1, 1)

    receive_all(0)
    pair_copy(0, h).start()

    rows_all = MOST * seq_count
    n, r = iota((rows_all, SLAB * seq_count), 0), iota((rows_all, SLAB * seq_count), 1)
    last = (r == SLAB * (n % seq_count) + SLAB - 1).astype(BF16)
    lines = dot(last, slabs[0, h])
    n, r = iota((rows_all, piece_w), 0), iota((rows_all, piece_w), 1)
    row_weight = jnp.sum(
        jnp.where(r == LANES * (n // seq_count), lines, 0.0), axis=1, keepdims=True
    )

    gate[...] = jnp.zeros_like(gate)
    up[...] = jnp.zeros_like(up)
    back[...] = jnp.zeros_like(back)

    def rows_of(a, i, x_ref):
        x = dot(unpack_rows(seq_count, i % PIECES), slabs[a, i // PIECES]).astype(BF16)
        x_ref[:, pl.ds(pl.multiple_of(i * piece_w, LANES), piece_w)] = x
        return x

    def forward_step(t, _):
        i = order(t)
        copies = weight_copies(i)
        x = rows_of(0, i, tokx_ref)
        copies[0].wait()
        gate[...] += dot(x, wg[i])
        copies[1].wait()
        up[...] += dot(x, wu[i])
        return 0

    def back_step(t, _):
        i = order(t)
        x = rows_of(1, i, gradx_ref)
        weight_copies(i)[2].wait()
        back[...] += col_contract(x, wd[i])
        return 0

    lax.fori_loop(0, PIECES, forward_step, 0)
    receive_all(1)
    pair_copy(1, h).start()
    pair_copy(0, 1 - h).wait_recv()
    lax.fori_loop(PIECES, 2 * PIECES, forward_step, 0)
    kept[0].start()
    lax.fori_loop(0, PIECES, back_step, 0)
    pair_copy(1, 1 - h).wait_recv()
    lax.fori_loop(PIECES, 2 * PIECES, back_step, 0)
    kept[1].start()

    gate_pre, up_pre = gate[...], up[...]
    sig = 1.0 / (1.0 + jnp.exp(-gate_pre))
    act = gate_pre * sig
    hidden_grad = row_weight * back[...]
    sc_ref[...] = (row_weight * act * up_pre).astype(BF16)
    dg_ref[...] = (
        hidden_grad * up_pre * (sig * (1.0 + gate_pre * (1.0 - sig)))
    ).astype(BF16)
    du_ref[...] = (hidden_grad * act).astype(BF16)
    for copy in kept[2:]:
        copy.start()

    cuts = packed.shape[0]
    cut = piece_w // cuts

    def terms(half, q, piece):
        i = half * PIECES + piece
        rows = pl.ds(pl.multiple_of(q * cut, SLAB), cut)
        return col_contract(dg_ref[...], wg[i, rows, :]) + col_contract(
            du_ref[...], wu[i, rows, :]
        )

    def part_copy(q):
        return pltpu.make_async_remote_copy(
            src_ref=sib_out.at[q],
            dst_ref=sib_in.at[q],
            send_sem=part_sem.at[0, q],
            recv_sem=part_sem.at[1, q],
            device_id=sib,
            device_id_type=MESH,
        )

    def reduce_copy(q, d):
        target = (c + d) % group
        return pltpu.make_async_remote_copy(
            src_ref=packed.at[
                q, pl.ds(pl.multiple_of(2 * SLAB * target, 2 * SLAB), 2 * SLAB), :
            ],
            dst_ref=red_in.at[q, d],
            send_sem=red_send.at[q, d],
            recv_sem=red_recv.at[q, d],
            device_id=(mine * group + target, h),
            device_id_type=MESH,
        )

    def far_step(q, _):
        for piece in range(PIECES):
            sib_out[q, piece] = terms(1 - h, q, piece).astype(BF16)
        part_copy(q).start()
        return 0

    def near_step(q, _):
        part_copy(q).wait_recv()
        acc = jnp.zeros((SLAB * seq_count, cut), F32)
        for piece in range(PIECES):
            both = terms(h, q, piece) + sib_in[q, piece].astype(F32)
            acc = acc + dot(pack_rows(seq_count, piece), both.astype(BF16))
        packed[q] = acc.astype(BF16)

        def send(d, _):
            reduce_copy(q, d).start()
            return 0

        lax.fori_loop(1, group, send, 0)
        return 0

    lax.fori_loop(0, cuts, far_step, 0)
    lax.fori_loop(0, cuts, near_step, 0)

    def final_copy(q):
        return pltpu.make_async_remote_copy(
            src_ref=fin_out.at[q],
            dst_ref=fin_in.at[q],
            send_sem=fin_sem.at[0, q],
            recv_sem=fin_sem.at[1, q],
            device_id=(mirror, h),
            device_id_type=MESH,
        )

    def sum_step(q, _):
        own = pl.ds(pl.multiple_of(2 * SLAB * c, 2 * SLAB), 2 * SLAB)
        total[q] = packed[q, own, :].astype(F32)

        def add(d, _):
            reduce_copy(q, d).wait_recv()
            total[q] += red_in[q, d].astype(F32)
            return 0

        lax.fori_loop(1, group, add, 0)
        away = pl.ds(pl.multiple_of(SLAB * other, SLAB), SLAB)
        fin_out[q] = total[q, away, :].astype(BF16)
        final_copy(q).start()
        return 0

    lax.fori_loop(0, cuts, sum_step, 0)

    stay = pl.ds(pl.multiple_of(SLAB * mine, SLAB), SLAB)
    for q in range(cuts):
        final_copy(q).wait_recv()
        near = total[q, stay, :].astype(BF16)
        far = fin_in[q]
        for piece in range(PIECES):
            value = dot(picker(place_mine, piece), near) + dot(
                picker(place_other, piece), far
            )
            out_ref[:, piece * piece_w + q * cut : piece * piece_w + (q + 1) * cut] = (
                value.astype(BF16)
            )

    for a in range(2):
        mirror_copy(a, own_rows).wait_send()
        pair_copy(a, h).wait_send()

    def sent(d, _):
        for a in range(2):
            for part in range(2):
                gather_copy(a, part, d, c).wait_send()
        for q in range(cuts):
            reduce_copy(q, d).wait_send()
        return 0

    lax.fori_loop(1, group, sent, 0)
    for q in range(cuts):
        part_copy(q).wait_send()
        final_copy(q).wait_send()
    for copy in kept:
        copy.wait()


def weight_grads(
    gt_ref, tokx_ref, gradx_ref, dg_ref, du_ref, sc_ref, gto_ref, gg_ref, gu_ref, gd_ref, sct
):
    @pl.when(pl.program_id(0) == 0)
    def _():
        gto_ref[...] = gt_ref[...]
        sct[...] = sc_ref[...].T

    xt = tokx_ref[...].T
    gg_ref[...] = dot(xt, dg_ref[...]).astype(BF16)
    gu_ref[...] = dot(xt, du_ref[...]).astype(BF16)
    gd_ref[...] = dot(sct[...], gradx_ref[...]).astype(BF16)


def paired_shards(group, tokens, out_grad, expert_ids, route_probs, w_gate, w_up, w_down):
    seq_count = EXP_WIN * group
    rows = MOST * seq_count
    width, hidden = w_gate.shape
    piece_w = width // (2 * PIECES)
    cuts = 2
    cut = piece_w // cuts
    dma = pltpu.SemaphoreType.DMA
    vmem = pl.BlockSpec(memory_space=pltpu.VMEM)
    hbm = pl.BlockSpec(memory_space=pl.ANY)
    small = jax.ShapeDtypeStruct((rows, hidden), BF16)
    wide = jax.ShapeDtypeStruct((rows, width), BF16)
    grad_tokens, d_gate, d_up, scaled, tok_x, grad_x = pl.pallas_call(
        functools.partial(layer_kernel, group),
        out_shape=(
            jax.ShapeDtypeStruct((tokens.shape[0], width // 2), BF16),
            small,
            small,
            small,
            wide,
            wide,
        ),
        in_specs=[vmem] * 4 + [hbm] * 3,
        out_specs=(vmem,) + (hbm,) * 5,
        scratch_shapes=[
            pltpu.VMEM((rows, hidden), BF16),
            pltpu.VMEM((rows, hidden), BF16),
            pltpu.VMEM((rows, hidden), BF16),
            pltpu.VMEM((rows, width), BF16),
            pltpu.VMEM((rows, width), BF16),
            pltpu.VMEM((2 * PIECES, piece_w, hidden), BF16),
            pltpu.VMEM((2 * PIECES, piece_w, hidden), BF16),
            pltpu.VMEM((2 * PIECES, hidden, piece_w), BF16),
            pltpu.VMEM((2, 2, SLAB * seq_count, piece_w), BF16),
            pltpu.VMEM((2, SLAB, piece_w), BF16),
            pltpu.VMEM((rows, hidden), F32),
            pltpu.VMEM((rows, hidden), F32),
            pltpu.VMEM((rows, hidden), F32),
            pltpu.VMEM((cuts, PIECES, rows, cut), BF16),
            pltpu.VMEM((cuts, PIECES, rows, cut), BF16),
            pltpu.VMEM((cuts, SLAB * seq_count, cut), BF16),
            pltpu.VMEM((cuts, group, 2 * SLAB, cut), BF16),
            pltpu.VMEM((cuts, 2 * SLAB, cut), F32),
            pltpu.VMEM((cuts, SLAB, cut), BF16),
            pltpu.VMEM((cuts, SLAB, cut), BF16),
            dma((3, 2 * PIECES)),
            dma((2, 2)),
            dma((2, 2, group)),
            dma((2, 2, group)),
            dma((2, 2)),
            dma((2, cuts)),
            dma((cuts, group)),
            dma((cuts, group)),
            dma((2, cuts)),
            dma((5,)),
        ],
        compiler_params=pltpu.CompilerParams(
            collective_id=0, has_side_effects=True, vmem_limit_bytes=60 * 2**20
        ),
        cost_estimate=pl.CostEstimate(
            flops=10 * rows * width * hidden,
            bytes_accessed=6 * width * hidden,
            transcendentals=rows * hidden,
        ),
    )(tokens, out_grad, expert_ids.T, route_probs.T, w_gate, w_up, w_down)

    step = piece_w // 2
    whole = pl.BlockSpec((rows, hidden), lambda i: (0, 0))
    strip = pl.BlockSpec((rows, step), lambda i: (0, i))
    whole_gt = pl.BlockSpec(grad_tokens.shape, lambda i: (0, 0))
    return pl.pallas_call(
        weight_grads,
        grid=(width // step,),
        out_shape=(
            jax.ShapeDtypeStruct(grad_tokens.shape, BF16),
            jax.ShapeDtypeStruct((width, hidden), BF16),
            jax.ShapeDtypeStruct((width, hidden), BF16),
            jax.ShapeDtypeStruct((hidden, width), BF16),
        ),
        in_specs=[whole_gt, strip, strip, whole, whole, whole],
        out_specs=(
            whole_gt,
            pl.BlockSpec((step, hidden), lambda i: (i, 0)),
            pl.BlockSpec((step, hidden), lambda i: (i, 0)),
            pl.BlockSpec((hidden, step), lambda i: (0, i)),
        ),
        scratch_shapes=[pltpu.VMEM((hidden, rows), BF16)],
        compiler_params=pltpu.CompilerParams(vmem_limit_bytes=62 * 2**20),
        cost_estimate=pl.CostEstimate(
            flops=6 * rows * width * hidden,
            bytes_accessed=6 * width * hidden,
            transcendentals=0,
        ),
    )(grad_tokens, tok_x, grad_x, d_gate, d_up, scaled)


def solution(mesh):
    paired = mesh.shape["hid"] == 2 and mesh.shape["seq"] % EXP_WIN == 0
    if paired:
        body = functools.partial(paired_shards, mesh.shape["seq"] // EXP_WIN)
    else:
        body = plain_shards
    return jax.shard_map(
        body,
        mesh=mesh,
        in_specs=(
            P("seq", None),
            P("seq", None),
            P("seq", None),
            P("seq", None),
            P(None, ("seq", "hid")),
            P(None, ("seq", "hid")),
            P(("seq", "hid"), None),
        ),
        out_specs=(
            P("seq", "hid"),
            P(None, ("seq", "hid")),
            P(None, ("seq", "hid")),
            P(("seq", "hid"), None),
        ),
        check_vma=False,
    )
```
